256 devices in a mesh: blk: 64 (over z, y, core), lag: 4 (over x).
Axes of the slice: x: 4, y: 4, z: 8, core: 2. Of those that a mesh axis runs over, the one named last changes fastest.
Arguments:
- excitation: bfloat16 [2, 65536, 128], P(None, 'blk'), may hold values from -6 to 6
- history: bfloat16 [16, 65536, 128], P('lag', 'blk'), may hold values from -6 to 6
- inter: bfloat16 [16, 64, 16, 4, 128, 128], P('lag', 'blk'), may hold values from -0.046875 to 0.046875
- src_lists: int32 [16, 64, 16, 4], P('lag', 'blk'), may hold values from 0 to 7, as said below
- dest_blocks: int32 [16, 64, 16], P('lag', 'blk'), may hold values from 0 to 511, as said below
- near: bfloat16 [512, 8, 128, 128], P('blk'), may hold values from -0.09375 to 0.09375
- diag_inverse: bfloat16 [512, 128, 128], P('blk'), may hold values from -0.5 to 0.5
- nbr_ids: int32 [512, 8], P('blk'), may hold values from 0 to 511, as said below
Outputs:
- currents: bfloat16 [2, 65536, 128], P(None, 'blk')
The draws below stay inside these ranges and needn't reach their ends.
Inputs may be any that keep to these rules, and one draw needn't show every extreme that they name: `dest_blocks`: for each source device and each group of 4 lags starting at a multiple of 4, at most 2 of its 64 entries lie on any one device (the two may name the same block), and exactly 2 entries lie on one device. `src_lists`: the 4 entries of one slot are distinct. `nbr_ids`: the 8 entries of a block are distinct, differ from the block itself, and lie on the block's device or one of the two beside it along blk.
All inputs are finite; a program needn't handle non-finite values.
Results may differ from the reference program's by a relative error of at most 0.019.
Values may be sent and summed in bfloat16 or wider, within the bound.
No kernel may reach another device: no remote copies, remote signals or barrier semaphores. Data moves between devices by JAX's collectives and lax.ppermute only.
A program may use at most 128 MiB of HBM per device.

```python
import jax
import jax.numpy as jnp
from jax import lax

B = 128
R = 128
BLK_DEV = 8
LAGS = 16
S = 16
Q = 4
K = 8
SWEEPS = 3
STEPS = 2
LAG_DEV = 4
NB = 512
UNK = 65536
CAP = 2
N_BLK = 64


def draw_dest_blocks(key, part):
    key = jax.random.fold_in(key, 11)
    groups = LAGS // LAG_DEV
    devices = NB // BLK_DEV
    item_count = LAG_DEV * S
    slots_all = devices * CAP

    def one_sender(sender_key):
        key_order, key_pick, key_mix, key_within = jax.random.split(sender_key, 4)
        scores = jax.random.permutation(key_order, slots_all)
        favored = jax.random.randint(key_pick, (), 0, devices)
        owners = jnp.arange(slots_all) // CAP
        scores = jnp.where(owners == favored, scores - slots_all, scores)
        chosen = jnp.argsort(scores)[:item_count] // CAP
        chosen = jax.random.permutation(key_mix, chosen)
        within = jax.random.randint(key_within, (item_count,), 0, BLK_DEV)
        return (chosen * BLK_DEV + within).astype(jnp.int32)
    sender_keys = jax.random.split(key, groups * devices)
    routing = jax.vmap(one_sender)(sender_keys).reshape(groups, devices, LAG_DEV, S)
    return jnp.transpose(routing, (0, 2, 1, 3)).reshape(LAGS, devices, S)


def draw_src_lists(key, part):
    key = jax.random.fold_in(key, 12)
    devices = NB // BLK_DEV
    row_count = LAGS * devices * S

    def one_slot(slot_key):
        return jax.random.permutation(slot_key, BLK_DEV)[:Q].astype(jnp.int32)
    slot_keys = jax.random.split(key, row_count)
    return jax.vmap(one_slot)(slot_keys).reshape(LAGS, devices, S, Q)


def draw_nbr_ids(key, part):
    key = jax.random.fold_in(key, 13)
    window = 3 * BLK_DEV

    def one_block(block_key, block):
        device = block // BLK_DEV
        base = (device - 1) * BLK_DEV
        candidate = base + jnp.arange(window)
        usable = (candidate >= 0) & (candidate < NB) & (candidate != block)
        scores = jax.random.permutation(block_key, window)
        scores = jnp.where(usable, scores, scores + window)
        picked = jnp.argsort(scores)[:K]
        return (base + picked).astype(jnp.int32)
    block_keys = jax.random.split(key, NB)
    return jax.vmap(one_block)(block_keys, jnp.arange(NB, dtype=jnp.int32))


def block_levels(rng, dims, shards, least, top_value):
    def one(position, parts):
        heights = jax.random.uniform(jax.random.fold_in(jax.random.fold_in(rng, 6), position), (parts,), jnp.float32, least / len(shards), top_value / len(shards))
        return jnp.repeat(jnp.exp(heights), dims[position] // parts).reshape((-1,) + (1,) * (len(dims) - position - 1))

    factor_of = one(*shards[0])
    for cut in shards[1:]:
        factor_of = factor_of * one(*cut)
    return factor_of


def normal_values(rng, shape, deviation, limit, cuts=(), kind=jnp.bfloat16):
    drawn = jax.random.normal(rng, shape, jnp.float32) * deviation
    if len(cuts) > 0:
        drawn = block_levels(rng, shape, cuts, -0.22, 0.18) * drawn
    return jnp.clip(drawn, min=-limit, max=limit).astype(kind)


def setup_inputs(seed: int = 0) -> dict:
    splits = jax.random.split(jax.random.key(seed), 9)
    return {
        "excitation": normal_values(splits[0], (STEPS, UNK, R), 1.0, 6.0, ((1, 64),)),
        "history": normal_values(splits[1], (LAGS, UNK, R), 1.0, 6.0, ((0, 4), (1, 64))),
        "inter": normal_values(splits[2], (LAGS, N_BLK, S, Q, B, B), (LAGS * S * Q * B // BLK_DEV) ** -0.5, 0.046875, ((0, 4), (1, 64))),
        "src_lists": draw_src_lists(jax.random.fold_in(splits[8], 71), 0),
        "dest_blocks": draw_dest_blocks(jax.random.fold_in(splits[8], 71), 0),
        "near": normal_values(splits[5], (NB, K, B, B), (4 * K * B) ** -0.5, 0.09375, ((0, 64),)),
        "diag_inverse": normal_values(splits[6], (NB, B, B), B ** -0.5, 0.5, ((0, 64),)),
        "nbr_ids": draw_nbr_ids(jax.random.fold_in(splits[8], 71), 0),
    }


def rounded(values):
    return lax.optimization_barrier(values.astype(jnp.bfloat16)).astype(jnp.float32)


def history_field(past, inter, source_ids, dest_blocks):
    def one_lag(running, pieces):
        current, coupling, chosen, targets = pieces
        picked = current[chosen].astype(jnp.float32)
        products = jnp.einsum("dsqab,dsqbr->dsar", coupling.astype(jnp.float32), picked)
        parcels = rounded(products).reshape(-1, B, R)
        running = running.at[targets.reshape(-1)].add(parcels)
        return running, None

    start = jnp.zeros((NB, B, R), jnp.float32)
    running, unused = lax.scan(one_lag, start, (past, inter, source_ids, dest_blocks))
    return running


def sweep_solve(drive, near, diag_inverse, nbr_ids):
    inverse = diag_inverse.astype(jnp.float32)
    coupling = near.astype(jnp.float32)
    current = jnp.einsum("gab,gbr->gar", inverse, rounded(drive)).astype(jnp.bfloat16)
    for sweep_index in range(SWEEPS):
        gathered = current[nbr_ids].astype(jnp.float32)
        pull = jnp.einsum("gmab,gmbr->gar", coupling, gathered)
        current = jnp.einsum("gab,gbr->gar", inverse, rounded(drive - pull)).astype(jnp.bfloat16)
    return current


def reference(excitation, history, inter, src_lists, dest_blocks, near, diag_inverse, nbr_ids):
    devices = NB // BLK_DEV
    past = history.reshape(LAGS, NB, B, R)
    offsets = jnp.arange(devices, dtype=jnp.int32) * BLK_DEV
    source_ids = (src_lists + offsets[None, :, None, None]).astype(jnp.int32)
    outputs = []
    for step_index in range(STEPS):
        field = history_field(past, inter, source_ids, dest_blocks)
        drive = excitation[step_index].reshape(NB, B, R).astype(jnp.float32) - field
        current = sweep_solve(drive, near, diag_inverse, nbr_ids)
        outputs.append(current.reshape(UNK, R))
        past = jnp.concatenate([current[None], past[:-1]], 0)
    return jnp.stack(outputs)
```

```python
import functools

import jax
import jax.numpy as jnp
from jax import lax
from jax.experimental import pallas as pl
from jax.experimental.pallas import tpu as pltpu
from jax.sharding import Mesh, PartitionSpec as P

SWEEPS = 3
NZ, NY, NC, NX = 8, 4, 2, 4
BLKS = 8
B = 128
RW = 32
BF = jnp.bfloat16
F32 = jnp.float32
VM = pl.BlockSpec(memory_space=pltpu.VMEM)
SM = pl.BlockSpec(memory_space=pltpu.SMEM)
ANY = pl.BlockSpec(memory_space=pl.ANY)
BLK = ("z", "y", "c")


def shape(*dims, dtype=BF):
    return jax.ShapeDtypeStruct(dims, dtype)


def cost(flops, bytes_accessed):
    return pl.CostEstimate(flops=int(flops), bytes_accessed=int(bytes_accessed), transcendentals=0)


def params(mib=32):
    return pltpu.CompilerParams(vmem_limit_bytes=mib * 1024 * 1024)


def shift(value, axis, distance):
    count = lax.axis_size(axis)
    return lax.ppermute(value, axis, [(i, (i + distance) % count) for i in range(count)])


def parcels_kernel(x_ref, src_ref, past_ref, inter_ref, *rest):
    outs, held = rest[:4], rest[4]
    k = pl.program_id(0)
    for j in range(16):
        total = None
        for i in range(4):
            source = src_ref[k * 64 + j * 4 + i]
            term = jnp.dot(inter_ref[0, j, i], past_ref[0, source], preferred_element_type=F32)
            total = term if total is None else total + term
        held[j] = total.T.astype(BF)
    for distance in range(4):
        start = pl.multiple_of(lax.rem(x_ref[0] + distance, NX) * RW, RW)
        outs[distance][...] = held[:, pl.ds(start, RW), :]


def parcels(x, sources, past, coupling):
    return pl.pallas_call(
        parcels_kernel,
        grid=(4,),
        in_specs=[
            SM,
            SM,
            pl.BlockSpec((1, BLKS, B, B), lambda k: (k, 0, 0, 0)),
            pl.BlockSpec((1, 16, 4, B, B), lambda k: (k, 0, 0, 0, 0)),
        ],
        out_specs=[pl.BlockSpec((16, RW, B), lambda k: (k, 0, 0))] * 4,
        out_shape=[shape(64, RW, B)] * 4,
        scratch_shapes=[pltpu.VMEM((16, B, B), BF)],
        compiler_params=params(),
        cost_estimate=cost(2 * 64 * 512 * B * B, 11 << 20),
    )(x, sources, past, coupling)


def place_kernel(count, per, parts, places_ref, *rest):
    ins, outs, dense, sems = rest[:count], rest[count : count + parts], rest[-2], rest[-1]
    dense[...] = jnp.zeros_like(dense)
    for n in range(count):

        def body(p, carry, n=n):
            at = places_ref[n * per + p]
            dense[at] = dense[at] + ins[n][p]
            return carry

        lax.fori_loop(0, per, body, 0, unroll=8)
    size = (dense.shape[0] - 1) // parts
    copies = [
        pltpu.make_async_copy(dense.at[pl.ds(n * size, size)], outs[n], sems.at[n])
        for n in range(parts)
    ]
    for copy in copies:
        copy.start()
    for copy in copies:
        copy.wait()


def place(places, buffers, blocks, parts):
    per = buffers[0].shape[0]
    count = len(buffers)
    return pl.pallas_call(
        functools.partial(place_kernel, count, per, parts),
        in_specs=[SM] + [VM] * count,
        out_specs=[ANY] * parts,
        out_shape=[shape(blocks // parts, RW, B)] * parts,
        scratch_shapes=[pltpu.VMEM((blocks + 1, RW, B), BF), pltpu.SemaphoreType.DMA((parts,))],
        compiler_params=params(),
        cost_estimate=cost(count * per * RW * B, (count * per + blocks) * RW * B * 2),
    )(places, *buffers)


def add_split_kernel(count, *refs):
    ins, outs = refs[:count], refs[count:]
    for n in range(NZ):
        part = pl.ds(n * BLKS, BLKS)
        total = ins[0][part].astype(F32)
        for value in ins[1:]:
            total = total + value[part].astype(F32)
        outs[n][...] = total.astype(BF)


def add_split(buffers):
    count = len(buffers)
    return pl.pallas_call(
        functools.partial(add_split_kernel, count),
        in_specs=[VM] * count,
        out_specs=[VM] * NZ,
        out_shape=[shape(BLKS, RW, B)] * NZ,
        compiler_params=params(),
        cost_estimate=cost(count * 64 * RW * B, (count + 1) * 64 * RW * B * 2),
    )(*buffers)


def first_solve_kernel(count, *refs):
    ins, (incident, inverse, drive_ref, current_ref) = refs[:count], refs[count:]
    total = ins[0][...].astype(F32)
    for value in ins[1:]:
        total = total + value[...].astype(F32)
    drive = incident[...].astype(F32) - total
    drive_ref[...] = drive
    rounded = drive.astype(BF)
    for g in range(BLKS):
        current_ref[g] = jnp.dot(rounded[g], inverse[g], preferred_element_type=F32).astype(BF)


def first_solve(pieces, incident, inverse):
    count = len(pieces)
    return pl.pallas_call(
        functools.partial(first_solve_kernel, count),
        in_specs=[VM] * (count + 2),
        out_specs=[VM] * 2,
        out_shape=[shape(BLKS, RW, B, dtype=F32), shape(BLKS, RW, B)],
        compiler_params=params(),
        cost_estimate=cost(2 * BLKS * RW * B * B, 1 << 20),
    )(*pieces, incident, inverse)


def sweep_kernel(ids_ref, left, own, right, drive_ref, near_ref, inverse, out_ref, held):
    held[0:BLKS] = left[...]
    held[BLKS : 2 * BLKS] = own[...]
    held[2 * BLKS : 3 * BLKS] = right[...]
    for g in range(BLKS):
        gathered = jnp.concatenate([held[ids_ref[g * 8 + m]] for m in range(8)], axis=1)
        pull = jnp.dot(gathered, near_ref[g], preferred_element_type=F32)
        rest = (drive_ref[g] - pull).astype(BF)
        out_ref[g] = jnp.dot(rest, inverse[g], preferred_element_type=F32).astype(BF)


def sweep(ids, left, own, right, drive, near, inverse):
    return pl.pallas_call(
        sweep_kernel,
        in_specs=[SM] + [VM] * 6,
        out_specs=VM,
        out_shape=shape(BLKS, RW, B),
        scratch_shapes=[pltpu.VMEM((3 * BLKS, RW, B), BF)],
        compiler_params=params(),
        cost_estimate=cost(2 * BLKS * RW * 9 * B * B, 3 << 20),
    )(ids, left, own, right, drive, near, inverse)


def late_parcels_kernel(src_ref, current, coupling, out_ref):
    for j in range(16):
        gathered = jnp.concatenate([current[src_ref[j * 4 + i]] for i in range(4)], axis=1)
        out_ref[j] = jnp.dot(gathered, coupling[j], preferred_element_type=F32).astype(BF)


def late_parcels(sources, current, coupling):
    return pl.pallas_call(
        late_parcels_kernel,
        in_specs=[SM, VM, VM],
        out_specs=VM,
        out_shape=shape(16, RW, B),
        compiler_params=params(),
        cost_estimate=cost(2 * 16 * RW * 512 * B, 3 << 20),
    )(sources, current, coupling)


def finish_kernel(x_ref, *refs):
    ins, out_ref, held = refs[:8], refs[8], refs[9]
    for step in range(2):
        for distance in range(4):
            start = pl.multiple_of(lax.rem(x_ref[0] + NX - distance, NX) * RW, RW)
            held[:, pl.ds(start, RW), :] = ins[step * 4 + distance][...]
        for g in range(BLKS):
            out_ref[step, g] = held[g].T


def finish(x, pieces):
    return pl.pallas_call(
        finish_kernel,
        in_specs=[SM] + [VM] * 8,
        out_specs=VM,
        out_shape=shape(2, BLKS, B, B),
        scratch_shapes=[pltpu.VMEM((BLKS, B, B), BF)],
        compiler_params=params(),
        cost_estimate=cost(1, 1 << 20),
    )(x, *pieces)


def spread(value, axis):
    return [value, shift(value, axis, 1), shift(value, axis, 2), shift(value, axis, -1)]


def per_device(excitation, history, inter, src_lists, dest_blocks, near, diag_inverse, nbr_ids):
    x, y, z, c = (lax.axis_index(name) for name in ("x", "y", "z", "c"))
    position = (z * NY + y) * NC + c
    x_scalar = x.astype(jnp.int32).reshape(1)
    past = history.reshape(4, BLKS, B, B)
    coupling = inter[:, 0]
    sources = src_lists[:, 0].reshape(256)

    sent = parcels(x_scalar, sources, past, coupling)
    older = lax.ppermute(past[3], "x", [(i, i + 1) for i in range(NX - 1)])
    later_past = jnp.concatenate([older[None], past[:3]], 0)

    meta = jnp.concatenate([dest_blocks[:, 0].reshape(64), sources[:64]])
    metas = jnp.stack(spread(meta, "x"))
    own_meta = lax.dynamic_index_in_dim(metas, x, 0, keepdims=False)
    late_sources = own_meta[64:]
    targets = metas[:, :64]
    targets = jnp.stack([targets, shift(targets, "c", 1)])
    late_targets = jnp.stack(spread(own_meta[:16], "y"))
    late_targets = jnp.stack([late_targets, shift(late_targets, "c", 1)])

    def place_of(target):
        device = target // BLKS
        inner = lax.rem(device // NC // NY - z + NZ, NZ) * BLKS + target % BLKS
        across = lax.rem(device // NC % NY - y + NY, NY)
        return device % NC == c, across, inner

    same, across, inner = place_of(targets)
    places = jnp.where(same, across * 64 + inner, 256).reshape(512)
    same, across, inner = place_of(late_targets)
    late_places = jnp.where(same & (across == 0), inner, 64).reshape(128)

    near_t = near.swapaxes(2, 3).reshape(BLKS, 8 * B, B)
    inverse_t = diag_inverse.swapaxes(1, 2)
    incident = excitation.reshape(2, BLKS, B, B).swapaxes(2, 3)
    incident = lax.dynamic_slice_in_dim(incident, x * RW, RW, axis=2)
    ids = (nbr_ids - (position - 1) * BLKS).reshape(64)

    def cross_x(sent):
        got = [sent[0], shift(sent[1], "x", 1), shift(sent[2], "x", 2), shift(sent[3], "x", -1)]
        return got + [shift(value, "c", 1) for value in got]

    def cross_y(sent):
        return [sent[0], shift(sent[1], "y", -3), shift(sent[2], "y", 2), shift(sent[3], "y", 3)]

    def cross_z(sent):
        return [sent[0]] + [shift(sent[n], "z", n) for n in range(1, NZ)]

    def sweeps(pieces, step):
        drive, current = first_solve(pieces, incident[step], inverse_t)
        ends = NZ * NY * NC - 1
        for _ in range(SWEEPS):
            left = lax.ppermute(current, BLK, [(i, i + 1) for i in range(ends)])
            right = lax.ppermute(current, BLK, [(i + 1, i) for i in range(ends)])
            current = sweep(ids, left, current, right, drive, near_t, inverse_t)
        return current

    got = cross_x(sent)
    dense = place(places, got, 256, 4)

    later_past, _ = lax.optimization_barrier((later_past, got[3]))
    later_sent = parcels(x_scalar, sources, later_past, coupling)
    later_got = cross_x(later_sent)
    late_coupling, _ = lax.optimization_barrier((coupling[0], later_got[3]))
    first = late_coupling
    copies = [first] + [lax.ppermute(first, "x", [(0, n)]) for n in range(1, NX)]
    late_coupling = copies[3]
    for n in range(NX - 2, -1, -1):
        late_coupling = jnp.where(x == n, copies[n], late_coupling)
    late_coupling = late_coupling.swapaxes(2, 3).reshape(16, 4 * B, B)

    halves = cross_y(dense)
    pieces = cross_z(add_split(halves))
    later_dense = place(places, later_got, 256, 4)
    later_dense, _ = lax.optimization_barrier((later_dense, halves[3]))
    later_pieces = cross_z(add_split(cross_y(later_dense)))

    current = sweeps(pieces, 0)
    outputs = spread(current, "x")

    late = spread(late_parcels(late_sources, current, late_coupling), "y")
    late = late + [shift(value, "c", 1) for value in late]
    (late_dense,) = place(late_places, late, 64, 1)
    late_pieces = cross_z([late_dense[n * BLKS : (n + 1) * BLKS] for n in range(NZ)])

    current = sweeps(later_pieces + late_pieces, 1)
    outputs = outputs + spread(current, "x")
    return finish(x_scalar, outputs).reshape(2, BLKS * B, B)


def solution(mesh):
    grid = Mesh(mesh.devices.reshape(NZ, NY, NC, NX), ("z", "y", "c", "x"))
    placed = (
        P(None, BLK, None),
        P("x", BLK, None),
        P("x", BLK, None, None, None, None),
        P("x", BLK, None, None),
        P("x", BLK, None),
        P(BLK, None, None, None),
        P(BLK, None, None),
        P(BLK, None),
    )
    return jax.shard_map(
        per_device, mesh=grid, in_specs=placed, out_specs=P(None, BLK, None), check_vma=False
    )
```

```python
import functools

import jax
import jax.numpy as jnp
from jax import lax
from jax.experimental import pallas as pl
from jax.experimental.pallas import tpu as pltpu
from jax.sharding import Mesh, PartitionSpec as P

SWEEPS = 3
NZ, NY, NC, NX = 8, 4, 2, 4
BLKS = 8
B = 128
RW = 32
BF = jnp.bfloat16
F32 = jnp.float32
VM = pl.BlockSpec(memory_space=pltpu.VMEM)
SM = pl.BlockSpec(memory_space=pltpu.SMEM)
ANY = pl.BlockSpec(memory_space=pl.ANY)
HBM = pl.BlockSpec(memory_space=pltpu.HBM)
BLK = ("z", "y", "c")


def shape(*dims, dtype=BF):
    return jax.ShapeDtypeStruct(dims, dtype)


def cost(flops, bytes_accessed):
    return pl.CostEstimate(flops=int(flops), bytes_accessed=int(bytes_accessed), transcendentals=0)


def params(mib=24):
    return pltpu.CompilerParams(vmem_limit_bytes=mib * 1024 * 1024)


def shift(value, axis, distance):
    count = lax.axis_size(axis)
    return lax.ppermute(value, axis, [(i, (i + distance) % count) for i in range(count)])


def parcels_kernel(first_ref, src_ref, past_ref, inter_ref, *rest):
    outs, held = rest[:-1], rest[-1]
    k = pl.program_id(0)
    for j in range(16):
        total = None
        for i in range(4):
            source = src_ref[k, 0, j, i]
            term = jnp.dot(inter_ref[0, j, i], past_ref[0, source], preferred_element_type=F32)
            total = term if total is None else total + term
        turned = total.T.astype(BF)
        if len(outs) == 1:
            for n in range(NX):
                outs[0][n, j] = turned[n * RW : (n + 1) * RW]
        else:
            held[j] = turned
    if len(outs) > 1:
        for distance in range(NX):
            start = pl.multiple_of(lax.rem(first_ref[0] + distance, NX) * RW, RW)
            outs[distance][...] = held[:, pl.ds(start, RW), :]


def parcels(first, sources, past, coupling, apart):
    whole = (pl.BlockSpec((NX, 16, RW, B), lambda k: (0, k, 0, 0)), shape(NX, 64, RW, B))
    part = (pl.BlockSpec((16, RW, B), lambda k: (k, 0, 0)), shape(64, RW, B))
    outs = [part] * NX if apart else [whole]
    return pl.pallas_call(
        parcels_kernel,
        grid=(4,),
        in_specs=[
            SM,
            SM,
            pl.BlockSpec((1, BLKS, B, B), lambda k: (k, 0, 0, 0)),
            pl.BlockSpec((1, 16, 4, B, B), lambda k: (k, 0, 0, 0, 0)),
        ],
        out_specs=[spec for spec, _ in outs],
        out_shape=[dims for _, dims in outs],
        scratch_shapes=[pltpu.VMEM((16, B, B), BF)],
        compiler_params=params(60),
        cost_estimate=cost(1, 1),
    )(first, sources, past, coupling)


def place_kernel(per, places_ref, *rest):
    ins, (out_ref, dense, sem) = rest[:-3], rest[-3:]
    dense[...] = jnp.zeros_like(dense)
    for n, values in enumerate(ins):

        def body(p, carry, n=n, values=values):
            at = places_ref[n * per + p]
            dense[at] = dense[at] + values[p]
            return carry

        lax.fori_loop(0, per, body, 0, unroll=8)
    copy = pltpu.make_async_copy(dense.at[pl.ds(0, 256)], out_ref, sem)
    copy.start()
    copy.wait()


def place(places, buffers):
    return pl.pallas_call(
        functools.partial(place_kernel, buffers[0].shape[0]),
        in_specs=[SM] + [VM] * len(buffers),
        out_specs=HBM,
        out_shape=shape(256, RW, B),
        scratch_shapes=[pltpu.VMEM((257, RW, B), BF), pltpu.SemaphoreType.DMA],
        compiler_params=params(),
        cost_estimate=cost(1, 1),
    )(places, *buffers)


def add_kernel(halves, out_ref):
    for n in range(NZ):
        total = halves[pl.ds(n * BLKS, BLKS)].astype(F32)
        for m in range(1, NY):
            total = total + halves[pl.ds(m * 64 + n * BLKS, BLKS)].astype(F32)
        out_ref[pl.ds(n * BLKS, BLKS)] = total.astype(BF)


def add(halves):
    return pl.pallas_call(
        add_kernel,
        in_specs=[VM],
        out_specs=VM,
        out_shape=shape(64, RW, B),
        compiler_params=params(),
        cost_estimate=cost(1, 1),
    )(halves)


def add_late_kernel(y_ref, places_ref, dense_ref, *rest):
    others, late, (out_ref, total, own, sem) = rest[:3], rest[3:5], rest[5:]
    start = pl.multiple_of(y_ref[0] * 64, 64)
    copy = pltpu.make_async_copy(dense_ref.at[pl.ds(start, 64)], own, sem)
    copy.start()
    for n in range(NZ):
        part = pl.ds(n * BLKS, BLKS)
        total[part] = sum(value[part].astype(F32) for value in others)
    copy.wait()
    for n in range(NZ):
        part = pl.ds(n * BLKS, BLKS)
        total[part] = total[part] + own[part].astype(F32)
    for n in range(2):

        def body(p, carry, n=n):
            at = places_ref[n * 64 + p]

            @pl.when(at < 64)
            def _():
                total[at] = total[at] + late[n][p].astype(F32)

            return carry

        lax.fori_loop(0, 64, body, 0, unroll=8)
    for n in range(NZ):
        part = pl.ds(n * BLKS, BLKS)
        out_ref[part] = total[part].astype(BF)


def add_late(y, places, dense, others, late):
    return pl.pallas_call(
        add_late_kernel,
        in_specs=[SM, SM, ANY] + [VM] * 5,
        out_specs=VM,
        out_shape=shape(64, RW, B),
        scratch_shapes=[
            pltpu.VMEM((64, RW, B), F32),
            pltpu.VMEM((64, RW, B), BF),
            pltpu.SemaphoreType.DMA,
        ],
        compiler_params=params(),
        cost_estimate=cost(1, 1),
    )(y, places, dense, *others, *late)


def total_of(ref, count):
    total = ref[pl.ds(0, BLKS)].astype(F32)
    for n in range(1, count):
        total = total + ref[pl.ds(n * BLKS, BLKS)].astype(F32)
    return total


def first_solve_kernel(pieces, incident, inverse, drive_ref, current_ref):
    drive = incident[...].astype(F32) - total_of(pieces, NZ)
    drive_ref[...] = drive
    rounded = drive.astype(BF)
    for g in range(BLKS):
        current_ref[g] = jnp.dot(rounded[g], inverse[g], preferred_element_type=F32).astype(BF)


def first_solve(pieces, incident, inverse):
    return pl.pallas_call(
        first_solve_kernel,
        in_specs=[VM] * 3,
        out_specs=[VM] * 2,
        out_shape=[shape(BLKS, RW, B, dtype=F32), shape(BLKS, RW, B)],
        compiler_params=params(),
        cost_estimate=cost(1, 1),
    )(pieces, incident, inverse)


def sweep_kernel(ids_ref, right, own, left, drive_ref, near_ref, inverse, out_ref, held):
    held[0:BLKS] = left[...]
    held[BLKS : 2 * BLKS] = own[...]
    held[2 * BLKS : 3 * BLKS] = right[...]
    for g in range(BLKS):
        gathered = jnp.concatenate([held[ids_ref[g * 8 + m]] for m in range(8)], axis=1)
        pull = jnp.dot(gathered, near_ref[g], preferred_element_type=F32)
        rest = (drive_ref[g] - pull).astype(BF)
        out_ref[g] = jnp.dot(rest, inverse[g], preferred_element_type=F32).astype(BF)


def sweep(ids, right, own, left, drive, near, inverse):
    return pl.pallas_call(
        sweep_kernel,
        in_specs=[SM] + [VM] * 6,
        out_specs=VM,
        out_shape=shape(BLKS, RW, B),
        scratch_shapes=[pltpu.VMEM((3 * BLKS, RW, B), BF)],
        compiler_params=params(),
        cost_estimate=cost(1, 1),
    )(ids, right, own, left, drive, near, inverse)


def late_parcels_kernel(x_ref, src_ref, current, *rest):
    (own, low, high, *far), (out_ref, coupling, sem) = rest[:5], rest[5:]
    x = x_ref[0]
    for half in range(2):
        part = pl.ds(half * 8, 8)
        choices = (own.at[part], low.at[part], far[half], high.at[part])
        for who, source in enumerate(choices):

            @pl.when(x == who)
            def _(part=part, half=half, source=source):
                pltpu.make_async_copy(source, coupling.at[part], sem.at[half]).start()

    for half in range(2):
        part = coupling.at[pl.ds(half * 8, 8)]
        pltpu.make_async_copy(part, part, sem.at[half]).wait()
        for j in range(half * 8, half * 8 + 8):
            gathered = jnp.concatenate([current[src_ref[j * 4 + i]] for i in range(4)], axis=1)
            parcel = jnp.dot(gathered, coupling[j], preferred_element_type=F32).astype(BF)
            for copy in range(NY):
                out_ref[copy * 16 + j] = parcel


def late_parcels(x, sources, current, couplings):
    return pl.pallas_call(
        late_parcels_kernel,
        in_specs=[SM, SM, VM] + [ANY] * 5,
        out_specs=VM,
        out_shape=shape(NY * 16, RW, B),
        scratch_shapes=[pltpu.VMEM((16, 4 * B, B), BF), pltpu.SemaphoreType.DMA((2,))],
        compiler_params=params(),
        cost_estimate=cost(1, 1),
    )(x, sources, current, *couplings)


def finish_kernel(x_ref, *refs):
    ins, out_ref, held = refs[:8], refs[8], refs[9]
    for step in range(2):
        for distance in range(4):
            start = pl.multiple_of(lax.rem(x_ref[0] + NX - distance, NX) * RW, RW)
            held[:, pl.ds(start, RW), :] = ins[step * 4 + distance][...]
        for g in range(BLKS):
            out_ref[step, g] = held[g].T


def finish(x, pieces):
    return pl.pallas_call(
        finish_kernel,
        in_specs=[SM] + [VM] * 8,
        out_specs=VM,
        out_shape=shape(2, BLKS, B, B),
        scratch_shapes=[pltpu.VMEM((BLKS, B, B), BF)],
        compiler_params=params(),
        cost_estimate=cost(1, 1),
    )(x, *pieces)


def spread(value, axis):
    return [value, shift(value, axis, 1), shift(value, axis, 2), shift(value, axis, -1)]


def after(value, *others):
    return lax.optimization_barrier((value,) + others)[0]


def exchange(value, axis):
    return lax.all_to_all(value, axis, split_axis=0, concat_axis=0, tiled=True)


def per_device(excitation, history, inter, src_lists, dest_blocks, near, diag_inverse, nbr_ids):
    x, y, z, c = (lax.axis_index(name) for name in ("x", "y", "z", "c"))
    position = (z * NY + y) * NC + c
    x_scalar = x.astype(jnp.int32).reshape(1)
    past = history.reshape(4, BLKS, B, B)
    coupling = inter[:, 0]

    meta = jnp.concatenate([dest_blocks[:, 0].reshape(64), src_lists[0, 0].reshape(64)])
    metas = exchange(jnp.broadcast_to(meta[None], (NX, 128)), "x")

    older = lax.ppermute(past[3], "x", [(i, i + 1) for i in range(NX - 1)])
    (sent,) = parcels(x_scalar, src_lists, past, coupling, False)
    sent = after(sent, older, metas)
    crossed = exchange(sent, "x")
    later_past = jnp.concatenate([after(older, sent)[None], past[:3]], 0)
    later_sent = parcels(x_scalar, src_lists, later_past, coupling, True)

    metas = after(metas, sent)
    metas = jnp.stack([metas, shift(metas, "c", 1)])
    late_sources = metas[0, 0, 64:]
    targets = metas[:, :, :64]
    late_targets = jnp.stack(spread(metas[:, 0, :16], "y"), axis=1)
    late_targets = jnp.take(late_targets, (y - jnp.arange(NY)) % NY, axis=1)

    def place_of(target):
        device = target // BLKS
        inner = device // NC // NY * BLKS + target % BLKS
        return device % NC == c, device // NC % NY, inner

    same, across, inner = place_of(targets)
    places = jnp.where(same, across * 64 + inner, 256).reshape(512)
    same, across, inner = place_of(late_targets)
    late_places = jnp.where(same & (across == y), inner, 64).reshape(128)

    by_distance = places.reshape(2, NX, 64)[:, (x - jnp.arange(NX)) % NX].reshape(512)
    newest = after(coupling[0], sent).swapaxes(2, 3).reshape(16, 4 * B, B)
    crossed = after(crossed, later_sent, places, by_distance, late_places, newest)
    crossed = crossed.reshape(256, RW, B)
    dense = place(places, [crossed, shift(crossed, "c", 1)])
    halves = exchange(dense, "y")
    later_sent = after(later_sent, dense)
    steps = (0, 1, 2, -1)
    later_crossed = [later_sent[0]] + [
        shift(later_sent[n], "x", steps[n]) for n in range(1, NX)
    ]

    near, diag_inverse, excitation = after((near, diag_inverse, excitation), dense)
    near_t = near.swapaxes(2, 3).reshape(BLKS, 8 * B, B)
    inverse_t = diag_inverse.swapaxes(1, 2)
    incident = excitation.reshape(2, BLKS, B, B).swapaxes(2, 3)
    incident = lax.dynamic_slice_in_dim(incident, x * RW, RW, axis=2)
    ids = (nbr_ids - (position - 1) * BLKS).reshape(64)

    def one_sweep(current, drive):
        ends = NZ * NY * NC - 1
        right = lax.ppermute(current, BLK, [(i + 1, i) for i in range(ends)])
        left = lax.ppermute(current, BLK, [(i, i + 1) for i in range(ends)])
        return sweep(ids, right, current, left, drive, near_t, inverse_t)

    later_own = shift(later_crossed[0], "c", 1)
    later_crossed = after(later_crossed, near_t, inverse_t, incident, ids, later_own)

    start = after(newest, later_crossed)
    low = lax.ppermute(start, "x", [(0, 1)])
    high = lax.ppermute(start, "x", [(0, 3)])
    halves = after(halves, later_crossed, later_own, near_t, inverse_t, incident, ids)
    summed = add(halves)
    pieces = exchange(summed, "z")

    later_other = [later_own] + [shift(value, "c", 1) for value in later_crossed[1:]]
    later_dense = place(by_distance, later_crossed + later_other)

    def other_part(distance):
        start = (y + distance) % NY * 64
        return lax.dynamic_slice_in_dim(later_dense, start, 64, axis=0)

    parts = [other_part(n) for n in range(1, NY)]
    pieces = after(pieces, later_dense, parts)
    later_halves = [shift(parts[n], "y", steps[n + 1]) for n in range(3)]

    drive, current = first_solve(pieces, incident[0], inverse_t)
    current = one_sweep(current, drive)
    current = after(current, later_halves[0], later_halves[2])
    current = one_sweep(current, drive)
    current, low, high = after((current, low, high), later_halves[1])
    far = [lax.ppermute(low[:8], "x", [(1, 2)]), lax.ppermute(high[8:], "x", [(3, 2)])]
    current = one_sweep(current, drive)
    outputs = spread(current, "x")

    couplings = after([newest, low, high] + far, current)
    late = exchange(late_parcels(x_scalar, late_sources, current, couplings), "y")
    y_scalar = y.astype(jnp.int32).reshape(1)
    late = [late, shift(late, "c", 1)]
    pieces = exchange(add_late(y_scalar, late_places, later_dense, later_halves, late), "z")
    pieces = after(pieces, outputs)
    drive, current = first_solve(pieces, incident[1], inverse_t)
    for _ in range(SWEEPS):
        current = one_sweep(current, drive)
    outputs = outputs + spread(current, "x")
    return finish(x_scalar, outputs).reshape(2, BLKS * B, B)


def solution(mesh):
    grid = Mesh(mesh.devices.reshape(NZ, NY, NC, NX), ("z", "y", "c", "x"))
    placed = (
        P(None, BLK, None),
        P("x", BLK, None),
        P("x", BLK, None, None, None, None),
        P("x", BLK, None, None),
        P("x", BLK, None),
        P(BLK, None, None, None),
        P(BLK, None, None),
        P(BLK, None),
    )
    return jax.shard_map(
        per_device, mesh=grid, in_specs=placed, out_specs=P(None, BLK, None), check_vma=False
    )
```

```python
import functools

import jax
import jax.numpy as jnp
from jax import lax
from jax.experimental import pallas as pl
from jax.experimental.pallas import tpu as pltpu
from jax.sharding import Mesh, PartitionSpec as P

SWEEPS = 3
NZ, NY, NC, NX = 8, 4, 2, 4
BLKS = 8
B = 128
RW = 32
BF = jnp.bfloat16
F32 = jnp.float32
VM = pl.BlockSpec(memory_space=pltpu.VMEM)
SM = pl.BlockSpec(memory_space=pltpu.SMEM)
ANY = pl.BlockSpec(memory_space=pl.ANY)
BLK = ("z", "y", "c")


def shape(*dims, dtype=BF):
    return jax.ShapeDtypeStruct(dims, dtype)


def cost(flops, bytes_accessed):
    return pl.CostEstimate(flops=int(flops), bytes_accessed=int(bytes_accessed), transcendentals=0)


def params(mib=24):
    return pltpu.CompilerParams(vmem_limit_bytes=mib * 1024 * 1024)


def shift(value, axis, distance):
    count = lax.axis_size(axis)
    return lax.ppermute(value, axis, [(i, (i + distance) % count) for i in range(count)])


def parcels_kernel(first_ref, src_ref, past_ref, inter_ref, *rest):
    outs, held = rest[:-1], rest[-1]
    k = pl.program_id(0)
    for j in range(16):
        total = None
        for i in range(4):
            source = src_ref[k, 0, i, j]
            term = jnp.dot(inter_ref[0, j, i], past_ref[0, source], preferred_element_type=F32)
            total = term if total is None else total + term
        turned = total.T.astype(BF)
        if len(outs) == 1:
            for n in range(NX):
                outs[0][n, j] = turned[n * RW : (n + 1) * RW]
        else:
            held[j] = turned
    if len(outs) > 1:
        for distance in range(NX):
            start = pl.multiple_of(lax.rem(first_ref[0] + distance, NX) * RW, RW)
            outs[distance][...] = held[:, pl.ds(start, RW), :]


def parcels(first, sources, past, coupling, apart):
    whole = (pl.BlockSpec((NX, 16, RW, B), lambda k: (0, k, 0, 0)), shape(NX, 64, RW, B))
    part = (pl.BlockSpec((16, RW, B), lambda k: (k, 0, 0)), shape(64, RW, B))
    outs = [part] * NX if apart else [whole]
    return pl.pallas_call(
        parcels_kernel,
        grid=(4,),
        in_specs=[
            SM,
            SM,
            pl.BlockSpec((1, BLKS, B, B), lambda k: (k, 0, 0, 0)),
            pl.BlockSpec((1, 16, 4, B, B), lambda k: (k, 0, 0, 0, 0)),
        ],
        out_specs=[spec for spec, _ in outs],
        out_shape=[dims for _, dims in outs],
        scratch_shapes=[pltpu.VMEM((16, B, B), BF)],
        compiler_params=params(60),
        cost_estimate=cost(1, 1),
    )(first, sources, past, coupling)


def place_kernel(count, places_ref, *rest):
    ins, (out_ref, held, dense, sems) = rest[:count], rest[count:]
    per = held.shape[1]
    arriving = [pltpu.make_async_copy(ins[n], held.at[n], sems.at[n]) for n in range(count)]
    for copy in arriving:
        copy.start()
    dense[...] = jnp.zeros_like(dense)
    for n in range(count):
        arriving[n].wait()

        def body(p, carry, n=n):
            at = places_ref[n * per + p]
            dense[at] = dense[at] + held[n, p]
            return carry

        lax.fori_loop(0, per, body, 0, unroll=8)
    leaving = pltpu.make_async_copy(dense.at[pl.ds(0, 256)], out_ref, sems.at[count])
    leaving.start()
    leaving.wait()


def place(places, buffers):
    count, per = len(buffers), buffers[0].shape[0]
    return pl.pallas_call(
        functools.partial(place_kernel, count),
        in_specs=[SM] + [ANY] * count,
        out_specs=ANY,
        out_shape=shape(256, RW, B),
        scratch_shapes=[
            pltpu.VMEM((count, per, RW, B), BF),
            pltpu.VMEM((257, RW, B), BF),
            pltpu.SemaphoreType.DMA((count + 1,)),
        ],
        compiler_params=params(60),
        cost_estimate=cost(1, 1),
    )(places, *buffers)


def add_kernel(halves, out_ref):
    for n in range(NZ):
        total = halves[pl.ds(n * BLKS, BLKS)].astype(F32)
        for m in range(1, NY):
            total = total + halves[pl.ds(m * 64 + n * BLKS, BLKS)].astype(F32)
        out_ref[pl.ds(n * BLKS, BLKS)] = total.astype(BF)


def add(halves):
    return pl.pallas_call(
        add_kernel,
        in_specs=[VM],
        out_specs=VM,
        out_shape=shape(64, RW, B),
        compiler_params=params(),
        cost_estimate=cost(1, 1),
    )(halves)


def add_late_kernel(places_ref, halves, first, second, out_ref, total):
    for n in range(NZ):
        part = pl.ds(n * BLKS, BLKS)
        total[part] = sum(halves[pl.ds(m * 64 + n * BLKS, BLKS)].astype(F32) for m in range(NY))
    for n, late in enumerate((first, second)):

        def body(p, carry, n=n, late=late):
            at = places_ref[n * 64 + p]

            @pl.when(at < 64)
            def _():
                total[at] = total[at] + late[p].astype(F32)

            return carry

        lax.fori_loop(0, 64, body, 0, unroll=8)
    for n in range(NZ):
        part = pl.ds(n * BLKS, BLKS)
        out_ref[part] = total[part].astype(BF)


def add_late(places, halves, first, second):
    return pl.pallas_call(
        add_late_kernel,
        in_specs=[SM] + [VM] * 3,
        out_specs=VM,
        out_shape=shape(64, RW, B),
        scratch_shapes=[pltpu.VMEM((64, RW, B), F32)],
        compiler_params=params(),
        cost_estimate=cost(1, 1),
    )(places, halves, first, second)


def total_of(ref, count):
    total = ref[pl.ds(0, BLKS)].astype(F32)
    for n in range(1, count):
        total = total + ref[pl.ds(n * BLKS, BLKS)].astype(F32)
    return total


def first_solve_kernel(pieces, incident, inverse, drive_ref, current_ref):
    drive = incident[...].astype(F32) - total_of(pieces, NZ)
    drive_ref[...] = drive
    rounded = drive.astype(BF)
    for g in range(BLKS):
        current_ref[g] = jnp.dot(rounded[g], inverse[g], preferred_element_type=F32).astype(BF)


def first_solve(pieces, incident, inverse):
    return pl.pallas_call(
        first_solve_kernel,
        in_specs=[VM] * 3,
        out_specs=[VM] * 2,
        out_shape=[shape(BLKS, RW, B, dtype=F32), shape(BLKS, RW, B)],
        compiler_params=params(),
        cost_estimate=cost(1, 1),
    )(pieces, incident, inverse)


def sweep_kernel(ids_ref, left, own, right, drive_ref, near_ref, inverse, out_ref, held):
    held[0:BLKS] = left[...]
    held[BLKS : 2 * BLKS] = own[...]
    held[2 * BLKS : 3 * BLKS] = right[...]
    for g in range(BLKS):
        gathered = jnp.concatenate([held[ids_ref[g * 8 + m]] for m in range(8)], axis=1)
        pull = jnp.dot(gathered, near_ref[g], preferred_element_type=F32)
        rest = (drive_ref[g] - pull).astype(BF)
        out_ref[g] = jnp.dot(rest, inverse[g], preferred_element_type=F32).astype(BF)


def sweep(ids, left, own, right, drive, near, inverse):
    return pl.pallas_call(
        sweep_kernel,
        in_specs=[SM] + [VM] * 6,
        out_specs=VM,
        out_shape=shape(BLKS, RW, B),
        scratch_shapes=[pltpu.VMEM((3 * BLKS, RW, B), BF)],
        compiler_params=params(),
        cost_estimate=cost(1, 1),
    )(ids, left, own, right, drive, near, inverse)


def gather_waves(x, pieces, whole):
    for distance, piece in enumerate(pieces):
        start = pl.multiple_of(lax.rem(x + NX - distance, NX) * RW, RW)
        whole[:, pl.ds(start, RW), :] = piece[...]


def late_parcels_kernel(x_ref, src_ref, *rest):
    pieces, coupling, outs, whole = rest[:4], rest[4], rest[5:9], rest[9]
    gather_waves(x_ref[0], pieces, whole)
    for j in range(16):
        gathered = jnp.concatenate([whole[src_ref[i * 16 + j]] for i in range(4)], axis=1)
        parcel = jnp.dot(gathered, coupling[j], preferred_element_type=F32).astype(BF)
        for n in range(NX):
            outs[n][j] = parcel[n * RW : (n + 1) * RW]


def late_parcels(x, sources, pieces, coupling):
    return pl.pallas_call(
        late_parcels_kernel,
        in_specs=[SM, SM] + [VM] * 5,
        out_specs=[VM] * NX,
        out_shape=[shape(16, RW, B)] * NX,
        scratch_shapes=[pltpu.VMEM((BLKS, B, B), BF)],
        compiler_params=params(),
        cost_estimate=cost(1, 1),
    )(x, sources, *pieces, coupling)


def finish_kernel(x_ref, *refs):
    ins, out_ref, held = refs[:8], refs[8], refs[9]
    for step in range(2):
        gather_waves(x_ref[0], ins[step * NX : (step + 1) * NX], held)
        for g in range(BLKS):
            out_ref[step, g] = held[g].T


def finish(x, pieces):
    return pl.pallas_call(
        finish_kernel,
        in_specs=[SM] + [VM] * 8,
        out_specs=VM,
        out_shape=shape(2, BLKS, B, B),
        scratch_shapes=[pltpu.VMEM((BLKS, B, B), BF)],
        compiler_params=params(),
        cost_estimate=cost(1, 1),
    )(x, *pieces)


def spread(value, axis):
    return [value, shift(value, axis, 1), shift(value, axis, 2), shift(value, axis, -1)]


def after(value, *others):
    return lax.optimization_barrier((value,) + others)[0]


def exchange(value, axis):
    return lax.all_to_all(value, axis, split_axis=0, concat_axis=0, tiled=True)


def per_device(excitation, history, inter, src_lists, dest_blocks, near, diag_inverse, nbr_ids):
    x, y, z, c = (lax.axis_index(name) for name in ("x", "y", "z", "c"))
    position = (z * NY + y) * NC + c
    x_scalar = x.astype(jnp.int32).reshape(1)
    past = history.reshape(4, BLKS, B, B)
    coupling = inter[:, 0]

    meta = jnp.concatenate([dest_blocks[:, 0].reshape(64), src_lists[0, 0].T.reshape(64)])
    metas = exchange(jnp.broadcast_to(meta[None], (NX, 128)), "x")

    older = shift(past[3], "x", 1)
    sources = src_lists.swapaxes(2, 3)
    (sent,) = parcels(x_scalar, sources, past, coupling, False)
    sent = after(sent, older, metas)
    crossed = exchange(sent, "x")
    older = jnp.where(x == 0, jnp.zeros_like(older), after(older, sent))
    later_past = jnp.concatenate([older[None], past[:3]], 0)
    later_sent = parcels(x_scalar, sources, later_past, coupling, True)

    metas = after(metas, sent)
    metas = jnp.stack([metas, shift(metas, "c", 1)])
    late_sources = metas[0, 0, 64:]
    targets = metas[:, :, :64]
    late_targets = jnp.stack(spread(metas[:, 0, :16], "y"), axis=1)
    late_targets = jnp.take(late_targets, (y - jnp.arange(NY)) % NY, axis=1)

    def place_of(target):
        device = target // BLKS
        inner = device // NC // NY * BLKS + target % BLKS
        return device % NC == c, device // NC % NY, inner

    same, across, inner = place_of(targets)
    places = jnp.where(same, across * 64 + inner, 256).reshape(512)
    same, across, inner = place_of(late_targets)
    late_places = jnp.where(same & (across == y), inner, 64).reshape(128)

    by_distance = places.reshape(2, NX, 64)[:, (x - jnp.arange(NX)) % NX].reshape(512)
    newest = after(coupling[0], sent).swapaxes(2, 3).reshape(16, 4 * B, B)
    crossed = after(crossed, later_sent, places, by_distance, late_places, newest)
    crossed = crossed.reshape(256, RW, B)
    dense = place(places, [crossed, shift(crossed, "c", 1)])
    halves = exchange(dense, "y")
    later_sent = after(later_sent, crossed)
    steps = (0, 1, 2, -1)
    later_crossed = [later_sent[0]] + [
        shift(later_sent[n], "x", steps[n]) for n in range(1, NX)
    ]

    near, diag_inverse, excitation = after((near, diag_inverse, excitation), dense)
    near_t = near.swapaxes(2, 3).reshape(BLKS, 8 * B, B)
    inverse_t = diag_inverse.swapaxes(1, 2)
    incident = excitation.reshape(2, BLKS, B, B).swapaxes(2, 3)
    incident = lax.dynamic_slice_in_dim(incident, x * RW, RW, axis=2)
    ids = (nbr_ids - (position - 1) * BLKS).reshape(64)

    def one_sweep(current, drive):
        right = shift(current, BLK, -1)
        left = shift(current, BLK, 1)
        return sweep(ids, left, current, right, drive, near_t, inverse_t)

    later_own = shift(later_crossed[0], "c", 1)
    later_crossed = after(later_crossed, near_t, inverse_t, incident, ids, later_own)

    halves = after(halves, later_crossed)
    summed = add(halves)
    pieces = exchange(summed, "z")

    later_other = [later_own] + [shift(value, "c", 1) for value in later_crossed[1:]]
    later_dense = place(by_distance, later_crossed + later_other)

    pieces = after(pieces, later_dense)
    drive, current = first_solve(pieces, incident[0], inverse_t)
    for _ in range(SWEEPS):
        current = one_sweep(current, drive)
    later_halves = exchange(after(later_dense, current), "y")
    outputs = spread(current, "x")

    late = late_parcels(x_scalar, late_sources, outputs, newest)
    late = [late[0], shift(late[1], "x", 1), shift(late[2], "x", 2), shift(late[3], "x", -1)]
    mine = late[3]
    for n in range(NX - 2, -1, -1):
        mine = jnp.where(x == n, late[n], mine)
    mine = jnp.broadcast_to(mine[None], (NY,) + mine.shape).reshape(NY * 16, RW, B)
    mine = exchange(after(mine, later_halves), "y")
    pieces = exchange(add_late(late_places, later_halves, mine, shift(mine, "c", 1)), "z")
    drive, current = first_solve(pieces, incident[1], inverse_t)
    for _ in range(SWEEPS):
        current = one_sweep(current, drive)
    outputs = outputs + spread(current, "x")
    return finish(x_scalar, outputs).reshape(2, BLKS * B, B)


def solution(mesh):
    grid = Mesh(mesh.devices.reshape(NZ, NY, NC, NX), ("z", "y", "c", "x"))
    placed = (
        P(None, BLK, None),
        P("x", BLK, None),
        P("x", BLK, None, None, None, None),
        P("x", BLK, None, None),
        P("x", BLK, None),
        P(BLK, None, None, None),
        P(BLK, None, None),
        P(BLK, None),
    )
    return jax.shard_map(
        per_device, mesh=grid, in_specs=placed, out_specs=P(None, BLK, None), check_vma=False
    )
```

```python
import functools

import jax
import jax.numpy as jnp
from jax import lax
from jax.experimental import pallas as pl
from jax.experimental.pallas import tpu as pltpu
from jax.sharding import Mesh, PartitionSpec as P

SWEEPS = 3
NZ, NY, NC, NX = 8, 4, 2, 4
BLKS = 8
B = 128
RW = 32
BF = jnp.bfloat16
F32 = jnp.float32
VM = pl.BlockSpec(memory_space=pltpu.VMEM)
SM = pl.BlockSpec(memory_space=pltpu.SMEM)
ANY = pl.BlockSpec(memory_space=pl.ANY)
BLK = ("z", "y", "c")


def shape(*dims, dtype=BF):
    return jax.ShapeDtypeStruct(dims, dtype)


def cost(flops, bytes_accessed):
    return pl.CostEstimate(flops=int(flops), bytes_accessed=int(bytes_accessed), transcendentals=0)


def params(mib=24):
    return pltpu.CompilerParams(vmem_limit_bytes=mib * 1024 * 1024)


def shift(value, axis, distance):
    count = lax.axis_size(axis)
    return lax.ppermute(value, axis, [(i, (i + distance) % count) for i in range(count)])


def parcels_kernel(first_ref, src_ref, past_ref, inter_ref, *rest):
    outs, held = rest[:-1], rest[-1]
    k = pl.program_id(0)
    for j in range(16):
        total = None
        for i in range(4):
            source = src_ref[k, 0, i, j]
            term = jnp.dot(inter_ref[0, j, i], past_ref[0, source], preferred_element_type=F32)
            total = term if total is None else total + term
        turned = total.T.astype(BF)
        if len(outs) == 1:
            for n in range(NX):
                outs[0][n, j] = turned[n * RW : (n + 1) * RW]
        else:
            held[j] = turned
    if len(outs) > 1:
        for distance in range(NX):
            start = pl.multiple_of(lax.rem(first_ref[0] + distance, NX) * RW, RW)
            outs[distance][...] = held[:, pl.ds(start, RW), :]


def parcels(first, sources, past, coupling, apart):
    whole = (pl.BlockSpec((NX, 16, RW, B), lambda k: (0, k, 0, 0)), shape(NX, 64, RW, B))
    part = (pl.BlockSpec((16, RW, B), lambda k: (k, 0, 0)), shape(64, RW, B))
    outs = [part] * NX if apart else [whole]
    return pl.pallas_call(
        parcels_kernel,
        grid=(4,),
        in_specs=[
            SM,
            SM,
            pl.BlockSpec((1, BLKS, B, B), lambda k: (k, 0, 0, 0)),
            pl.BlockSpec((1, 16, 4, B, B), lambda k: (k, 0, 0, 0, 0)),
        ],
        out_specs=[spec for spec, _ in outs],
        out_shape=[dims for _, dims in outs],
        scratch_shapes=[pltpu.VMEM((16, B, B), BF)],
        compiler_params=params(60),
        cost_estimate=cost(1, 1),
    )(first, sources, past, coupling)


def place_kernel(count, places_ref, *rest):
    ins, (out_ref, dense, sem) = rest[:count], rest[count:]
    per = ins[0].shape[0]
    dense[...] = jnp.zeros_like(dense)
    for n, values in enumerate(ins):

        def body(p, carry, n=n, values=values):
            at = places_ref[n * per + p]
            dense[at] = dense[at] + values[p]
            return carry

        lax.fori_loop(0, per, body, 0, unroll=8)
    copy = pltpu.make_async_copy(dense.at[pl.ds(0, 256)], out_ref, sem)
    copy.start()
    copy.wait()


def place(places, buffers):
    count = len(buffers)
    return pl.pallas_call(
        functools.partial(place_kernel, count),
        in_specs=[SM] + [VM] * count,
        out_specs=ANY,
        out_shape=shape(256, RW, B),
        scratch_shapes=[pltpu.VMEM((257, RW, B), BF), pltpu.SemaphoreType.DMA],
        compiler_params=params(),
        cost_estimate=cost(1, 1),
    )(places, *buffers)


def add_kernel(halves, out_ref):
    for n in range(NZ):
        total = halves[pl.ds(n * BLKS, BLKS)].astype(F32)
        for m in range(1, NY):
            total = total + halves[pl.ds(m * 64 + n * BLKS, BLKS)].astype(F32)
        out_ref[pl.ds(n * BLKS, BLKS)] = total.astype(BF)


def add(halves):
    return pl.pallas_call(
        add_kernel,
        in_specs=[VM],
        out_specs=VM,
        out_shape=shape(64, RW, B),
        compiler_params=params(),
        cost_estimate=cost(1, 1),
    )(halves)


def add_late_kernel(places_ref, halves, first, second, out_ref, total):
    for n in range(NZ):
        part = pl.ds(n * BLKS, BLKS)
        total[part] = sum(halves[pl.ds(m * 64 + n * BLKS, BLKS)].astype(F32) for m in range(NY))
    for n, late in enumerate((first, second)):

        def body(p, carry, n=n, late=late):
            at = places_ref[n * 64 + p]

            @pl.when(at < 64)
            def _():
                total[at] = total[at] + late[p].astype(F32)

            return carry

        lax.fori_loop(0, 64, body, 0, unroll=8)
    for n in range(NZ):
        part = pl.ds(n * BLKS, BLKS)
        out_ref[part] = total[part].astype(BF)


def add_late(places, halves, first, second):
    return pl.pallas_call(
        add_late_kernel,
        in_specs=[SM] + [VM] * 3,
        out_specs=VM,
        out_shape=shape(64, RW, B),
        scratch_shapes=[pltpu.VMEM((64, RW, B), F32)],
        compiler_params=params(),
        cost_estimate=cost(1, 1),
    )(places, halves, first, second)


def total_of(ref, count):
    total = ref[pl.ds(0, BLKS)].astype(F32)
    for n in range(1, count):
        total = total + ref[pl.ds(n * BLKS, BLKS)].astype(F32)
    return total


def first_solve_kernel(pieces, incident, inverse, drive_ref, current_ref):
    drive = incident[...].astype(F32) - total_of(pieces, NZ)
    drive_ref[...] = drive
    rounded = drive.astype(BF)
    for g in range(BLKS):
        current_ref[g] = jnp.dot(rounded[g], inverse[g], preferred_element_type=F32).astype(BF)


def first_solve(pieces, incident, inverse):
    return pl.pallas_call(
        first_solve_kernel,
        in_specs=[VM] * 3,
        out_specs=[VM] * 2,
        out_shape=[shape(BLKS, RW, B, dtype=F32), shape(BLKS, RW, B)],
        compiler_params=params(),
        cost_estimate=cost(1, 1),
    )(pieces, incident, inverse)


def sweep_kernel(ids_ref, right, own, left, drive_ref, near_ref, inverse, out_ref, held):
    held[0:BLKS] = left[...]
    held[BLKS : 2 * BLKS] = own[...]
    held[2 * BLKS : 3 * BLKS] = right[...]
    for g in range(BLKS):
        gathered = jnp.concatenate([held[ids_ref[g * 8 + m]] for m in range(8)], axis=1)
        pull = jnp.dot(gathered, near_ref[g], preferred_element_type=F32)
        rest = (drive_ref[g] - pull).astype(BF)
        out_ref[g] = jnp.dot(rest, inverse[g], preferred_element_type=F32).astype(BF)


def sweep(ids, right, own, left, drive, near, inverse):
    return pl.pallas_call(
        sweep_kernel,
        in_specs=[SM] + [VM] * 6,
        out_specs=VM,
        out_shape=shape(BLKS, RW, B),
        scratch_shapes=[pltpu.VMEM((3 * BLKS, RW, B), BF)],
        compiler_params=params(),
        cost_estimate=cost(1, 1),
    )(ids, right, own, left, drive, near, inverse)


def gather_waves(x, pieces, whole):
    for distance, piece in enumerate(pieces):
        start = pl.multiple_of(lax.rem(x + NX - distance, NX) * RW, RW)
        whole[:, pl.ds(start, RW), :] = piece[...]


def late_parcels_kernel(x_ref, src_ref, *rest):
    pieces, coupling, outs, whole = rest[:4], rest[4], rest[5:9], rest[9]
    gather_waves(x_ref[0], pieces, whole)
    for j in range(16):
        gathered = jnp.concatenate([whole[src_ref[0, 0, i, j]] for i in range(4)], axis=1)
        parcel = jnp.dot(gathered, coupling[j], preferred_element_type=F32).astype(BF)
        for n in range(NX):
            outs[n][j] = parcel[n * RW : (n + 1) * RW]


def late_parcels(x, sources, pieces, coupling):
    return pl.pallas_call(
        late_parcels_kernel,
        in_specs=[SM, SM] + [VM] * 5,
        out_specs=[VM] * NX,
        out_shape=[shape(16, RW, B)] * NX,
        scratch_shapes=[pltpu.VMEM((BLKS, B, B), BF)],
        compiler_params=params(),
        cost_estimate=cost(1, 1),
    )(x, sources, *pieces, coupling)


def finish_kernel(x_ref, *refs):
    ins, out_ref, held = refs[:8], refs[8], refs[9]
    for step in range(2):
        gather_waves(x_ref[0], ins[step * NX : (step + 1) * NX], held)
        for g in range(BLKS):
            out_ref[step, g] = held[g].T


def finish(x, pieces):
    return pl.pallas_call(
        finish_kernel,
        in_specs=[SM] + [VM] * 8,
        out_specs=VM,
        out_shape=shape(2, BLKS, B, B),
        scratch_shapes=[pltpu.VMEM((BLKS, B, B), BF)],
        compiler_params=params(),
        cost_estimate=cost(1, 1),
    )(x, *pieces)


def spread(value, axis):
    return [value, shift(value, axis, 1), shift(value, axis, 2), shift(value, axis, -1)]


def after(value, *others):
    return lax.optimization_barrier((value,) + others)[0]


def exchange(value, axis):
    return lax.all_to_all(value, axis, split_axis=0, concat_axis=0, tiled=True)


def per_device(excitation, history, inter, src_lists, dest_blocks, near, diag_inverse, nbr_ids):
    x, y, z, c = (lax.axis_index(name) for name in ("x", "y", "z", "c"))
    position = (z * NY + y) * NC + c
    x_scalar = x.astype(jnp.int32).reshape(1)
    past = history.reshape(4, BLKS, B, B)
    coupling = inter[:, 0]

    lists = jnp.broadcast_to(dest_blocks[:, 0][None], (NX, 4, 16))
    metas = exchange(lists, "x")

    older = shift(past[3], "x", 1)
    sources = src_lists.swapaxes(2, 3)
    (sent,) = parcels(x_scalar, sources, past, coupling, False)
    sent = after(sent, older, metas)
    crossed = exchange(sent, "x")
    older = jnp.where(x == 0, jnp.zeros_like(older), after(older, sent))
    later_past = jnp.concatenate([older[None], past[:3]], 0)
    later_sent = parcels(x_scalar, sources, later_past, coupling, True)

    metas = after(metas, sent).reshape(NX, 64)
    targets = jnp.stack([metas, shift(metas, "c", 1)])
    late_targets = jnp.stack(spread(targets[:, 0, :16], "y"), axis=1)
    late_targets = jnp.take(late_targets, (y - jnp.arange(NY)) % NY, axis=1)

    def place_of(target):
        device = target // BLKS
        inner = device // NC // NY * BLKS + target % BLKS
        return device % NC == c, device // NC % NY, inner

    same, across, inner = place_of(targets)
    places = jnp.where(same, across * 64 + inner, 256).reshape(512)
    same, across, inner = place_of(late_targets)
    late_places = jnp.where(same & (across == y), inner, 64).reshape(128)

    by_distance = places.reshape(2, NX, 64)[:, (x - jnp.arange(NX)) % NX].reshape(512)
    newest = after(coupling, sent)[0].swapaxes(2, 3).reshape(16, 4 * B, B)
    crossed = after(crossed, later_sent, places, by_distance, late_places, newest)
    crossed = crossed.reshape(256, RW, B)
    dense = place(places, [crossed, shift(crossed, "c", 1)])
    halves = exchange(dense, "y")
    later_sent = after(later_sent, crossed)
    steps = (0, 1, 2, -1)
    later_crossed = [later_sent[0]] + [
        shift(later_sent[n], "x", steps[n]) for n in range(1, NX)
    ]

    near, diag_inverse, excitation = after((near, diag_inverse, excitation), dense)
    near_t = near.swapaxes(2, 3).reshape(BLKS, 8 * B, B)
    inverse_t = diag_inverse.swapaxes(1, 2)
    incident = excitation.reshape(2, BLKS, B, B).swapaxes(2, 3)
    incident = lax.dynamic_slice_in_dim(incident, x * RW, RW, axis=2)
    ids = (nbr_ids - (position - 1) * BLKS).reshape(64)

    def one_sweep(current, drive):
        right = shift(current, BLK, -1)
        left = shift(current, BLK, 1)
        return sweep(ids, right, current, left, drive, near_t, inverse_t)

    later_own = shift(later_crossed[0], "c", 1)
    later_crossed = after(later_crossed, near_t, inverse_t, incident, ids, later_own)

    halves = after(halves, near_t, inverse_t, incident, ids)
    summed = add(halves)
    pieces = exchange(summed, "z")

    later_other = [later_own] + [shift(value, "c", 1) for value in later_crossed[1:]]
    later_dense = place(by_distance, later_crossed + later_other)

    pieces = after(pieces, later_dense)
    drive, current = first_solve(pieces, incident[0], inverse_t)
    for _ in range(SWEEPS):
        current = one_sweep(current, drive)
    later_halves = exchange(after(later_dense, current), "y")
    outputs = spread(current, "x")

    late = late_parcels(x_scalar, sources, outputs, newest)
    late = [late[0], shift(late[1], "x", 1), shift(late[2], "x", 2), shift(late[3], "x", -1)]
    mine = late[3]
    for n in range(NX - 2, -1, -1):
        mine = jnp.where(x == n, late[n], mine)
    mine = jnp.broadcast_to(mine[None], (NY,) + mine.shape).reshape(NY * 16, RW, B)
    mine = exchange(after(mine, later_halves), "y")
    pieces = exchange(add_late(late_places, later_halves, mine, shift(mine, "c", 1)), "z")
    drive, current = first_solve(pieces, incident[1], inverse_t)
    for _ in range(SWEEPS):
        current = one_sweep(current, drive)
    outputs = outputs + spread(current, "x")
    return finish(x_scalar, outputs).reshape(2, BLKS * B, B)


def solution(mesh):
    grid = Mesh(mesh.devices.reshape(NZ, NY, NC, NX), ("z", "y", "c", "x"))
    placed = (
        P(None, BLK, None),
        P("x", BLK, None),
        P("x", BLK, None, None, None, None),
        P("x", BLK, None, None),
        P("x", BLK, None),
        P(BLK, None, None, None),
        P(BLK, None, None),
        P(BLK, None),
    )
    return jax.shard_map(
        per_device, mesh=grid, in_specs=placed, out_specs=P(None, BLK, None), check_vma=False
    )
```

```python
import functools

import jax
import jax.numpy as jnp
from jax import lax
from jax.experimental import pallas as pl
from jax.experimental.pallas import tpu as pltpu
from jax.sharding import Mesh, PartitionSpec as P

SWEEPS = 3
NZ, NY, NC, NX = 8, 4, 2, 4
BLKS = 8
B = 128
RW = 32
BF = jnp.bfloat16
F32 = jnp.float32
VM = pl.BlockSpec(memory_space=pltpu.VMEM)
SM = pl.BlockSpec(memory_space=pltpu.SMEM)
ANY = pl.BlockSpec(memory_space=pl.ANY)
BLK = ("z", "y", "c")


def shape(*dims, dtype=BF):
    return jax.ShapeDtypeStruct(dims, dtype)


def cost(flops, bytes_accessed):
    return pl.CostEstimate(flops=int(flops), bytes_accessed=int(bytes_accessed), transcendentals=0)


def params(mib=24):
    return pltpu.CompilerParams(vmem_limit_bytes=mib * 1024 * 1024)


def shift(value, axis, distance):
    count = lax.axis_size(axis)
    return lax.ppermute(value, axis, [(i, (i + distance) % count) for i in range(count)])


def parcels_kernel(first_ref, src_ref, past_ref, inter_ref, *rest):
    outs, held = rest[:-1], rest[-1]
    k = pl.program_id(0)
    for j in range(16):
        total = None
        for i in range(4):
            source = src_ref[k, 0, i, j]
            term = jnp.dot(inter_ref[0, j, i], past_ref[0, source], preferred_element_type=F32)
            total = term if total is None else total + term
        turned = total.T.astype(BF)
        if len(outs) == 1:
            for n in range(NX):
                outs[0][n, j] = turned[n * RW : (n + 1) * RW]
        else:
            held[j] = turned
    if len(outs) > 1:
        for distance in range(NX):
            start = pl.multiple_of(lax.rem(first_ref[0] + distance, NX) * RW, RW)
            outs[distance][...] = held[:, pl.ds(start, RW), :]


def parcels(first, sources, past, coupling, apart):
    whole = (pl.BlockSpec((NX, 16, RW, B), lambda k: (0, k, 0, 0)), shape(NX, 64, RW, B))
    part = (pl.BlockSpec((16, RW, B), lambda k: (k, 0, 0)), shape(64, RW, B))
    outs = [part] * NX if apart else [whole]
    return pl.pallas_call(
        parcels_kernel,
        grid=(4,),
        in_specs=[
            SM,
            SM,
            pl.BlockSpec((1, BLKS, B, B), lambda k: (k, 0, 0, 0)),
            pl.BlockSpec((1, 16, 4, B, B), lambda k: (k, 0, 0, 0, 0)),
        ],
        out_specs=[spec for spec, _ in outs],
        out_shape=[dims for _, dims in outs],
        scratch_shapes=[pltpu.VMEM((16, B, B), BF)],
        compiler_params=params(60),
        cost_estimate=cost(1, 1),
    )(first, sources, past, coupling)


def place_kernel(count, places_ref, *rest):
    ins, (out_ref, dense, sem) = rest[:count], rest[count:]
    per = ins[0].shape[0]
    dense[...] = jnp.zeros_like(dense)
    for n, values in enumerate(ins):

        def body(p, carry, n=n, values=values):
            at = places_ref[n * per + p]
            dense[at] = dense[at] + values[p]
            return carry

        lax.fori_loop(0, per, body, 0, unroll=8)
    copy = pltpu.make_async_copy(dense.at[pl.ds(0, 256)], out_ref, sem)
    copy.start()
    copy.wait()


def place(places, buffers):
    count = len(buffers)
    return pl.pallas_call(
        functools.partial(place_kernel, count),
        in_specs=[SM] + [VM] * count,
        out_specs=ANY,
        out_shape=shape(256, RW, B),
        scratch_shapes=[pltpu.VMEM((257, RW, B), BF), pltpu.SemaphoreType.DMA],
        compiler_params=params(),
        cost_estimate=cost(1, 1),
    )(places, *buffers)


def add_kernel(halves, out_ref):
    for n in range(NZ):
        total = halves[pl.ds(n * BLKS, BLKS)].astype(F32)
        for m in range(1, NY):
            total = total + halves[pl.ds(m * 64 + n * BLKS, BLKS)].astype(F32)
        out_ref[pl.ds(n * BLKS, BLKS)] = total.astype(BF)


def add(halves):
    return pl.pallas_call(
        add_kernel,
        in_specs=[VM],
        out_specs=VM,
        out_shape=shape(64, RW, B),
        compiler_params=params(),
        cost_estimate=cost(1, 1),
    )(halves)


def add_late_kernel(places_ref, halves, *rest):
    lates, (out_ref, total) = rest[:-2], rest[-2:]
    for n in range(NZ):
        part = pl.ds(n * BLKS, BLKS)
        total[part] = sum(halves[pl.ds(m * 64 + n * BLKS, BLKS)].astype(F32) for m in range(NY))
    for n, late in enumerate(lates):

        def body(p, carry, n=n, late=late):
            at = places_ref[n * 16 + p]

            @pl.when(at < 64)
            def _():
                total[at] = total[at] + late[p].astype(F32)

            return carry

        lax.fori_loop(0, 16, body, 0, unroll=8)
    for n in range(NZ):
        part = pl.ds(n * BLKS, BLKS)
        out_ref[part] = total[part].astype(BF)


def add_late(places, halves, lates):
    return pl.pallas_call(
        add_late_kernel,
        in_specs=[SM] + [VM] * (1 + len(lates)),
        out_specs=VM,
        out_shape=shape(64, RW, B),
        scratch_shapes=[pltpu.VMEM((64, RW, B), F32)],
        compiler_params=params(),
        cost_estimate=cost(1, 1),
    )(places, halves, *lates)


def total_of(ref, count):
    total = ref[pl.ds(0, BLKS)].astype(F32)
    for n in range(1, count):
        total = total + ref[pl.ds(n * BLKS, BLKS)].astype(F32)
    return total


def first_solve_kernel(pieces, incident, inverse, drive_ref, current_ref):
    drive = incident[...].astype(F32) - total_of(pieces, NZ)
    drive_ref[...] = drive
    rounded = drive.astype(BF)
    for g in range(BLKS):
        current_ref[g] = jnp.dot(rounded[g], inverse[g], preferred_element_type=F32).astype(BF)


def first_solve(pieces, incident, inverse):
    return pl.pallas_call(
        first_solve_kernel,
        in_specs=[VM] * 3,
        out_specs=[VM] * 2,
        out_shape=[shape(BLKS, RW, B, dtype=F32), shape(BLKS, RW, B)],
        compiler_params=params(),
        cost_estimate=cost(1, 1),
    )(pieces, incident, inverse)


def sweep_kernel(ids_ref, right, own, left, drive_ref, near_ref, inverse, out_ref, held):
    held[0:BLKS] = left[...]
    held[BLKS : 2 * BLKS] = own[...]
    held[2 * BLKS : 3 * BLKS] = right[...]
    for g in range(BLKS):
        gathered = jnp.concatenate([held[ids_ref[g * 8 + m]] for m in range(8)], axis=1)
        pull = jnp.dot(gathered, near_ref[g], preferred_element_type=F32)
        rest = (drive_ref[g] - pull).astype(BF)
        out_ref[g] = jnp.dot(rest, inverse[g], preferred_element_type=F32).astype(BF)


def sweep(ids, right, own, left, drive, near, inverse):
    return pl.pallas_call(
        sweep_kernel,
        in_specs=[SM] + [VM] * 6,
        out_specs=VM,
        out_shape=shape(BLKS, RW, B),
        scratch_shapes=[pltpu.VMEM((3 * BLKS, RW, B), BF)],
        compiler_params=params(),
        cost_estimate=cost(1, 1),
    )(ids, right, own, left, drive, near, inverse)


def gather_waves(x, pieces, whole):
    for distance, piece in enumerate(pieces):
        start = pl.multiple_of(lax.rem(x + NX - distance, NX) * RW, RW)
        whole[:, pl.ds(start, RW), :] = piece[...]


def late_parcels_kernel(x_ref, src_ref, *rest):
    pieces, coupling, outs, whole = rest[:4], rest[4], rest[5:9], rest[9]
    gather_waves(x_ref[0], pieces, whole)
    for j in range(16):
        gathered = jnp.concatenate([whole[src_ref[0, 0, i, j]] for i in range(4)], axis=1)
        parcel = jnp.dot(gathered, coupling[j], preferred_element_type=F32).astype(BF)
        for n in range(NX):
            outs[n][j] = parcel[n * RW : (n + 1) * RW]


def late_parcels(x, sources, pieces, coupling):
    return pl.pallas_call(
        late_parcels_kernel,
        in_specs=[SM, SM] + [VM] * 5,
        out_specs=[VM] * NX,
        out_shape=[shape(16, RW, B)] * NX,
        scratch_shapes=[pltpu.VMEM((BLKS, B, B), BF)],
        compiler_params=params(),
        cost_estimate=cost(1, 1),
    )(x, sources, *pieces, coupling)


def finish_kernel(x_ref, *refs):
    ins, out_ref, held = refs[:8], refs[8], refs[9]
    for step in range(2):
        gather_waves(x_ref[0], ins[step * NX : (step + 1) * NX], held)
        for g in range(BLKS):
            out_ref[step, g] = held[g].T


def finish(x, pieces):
    return pl.pallas_call(
        finish_kernel,
        in_specs=[SM] + [VM] * 8,
        out_specs=VM,
        out_shape=shape(2, BLKS, B, B),
        scratch_shapes=[pltpu.VMEM((BLKS, B, B), BF)],
        compiler_params=params(),
        cost_estimate=cost(1, 1),
    )(x, *pieces)


def spread(value, axis):
    return [value, shift(value, axis, 1), shift(value, axis, 2), shift(value, axis, -1)]


def after(value, *others):
    return lax.optimization_barrier((value,) + others)[0]


def exchange(value, axis):
    return lax.all_to_all(value, axis, split_axis=0, concat_axis=0, tiled=True)


def per_device(excitation, history, inter, src_lists, dest_blocks, near, diag_inverse, nbr_ids):
    x, y, z, c = (lax.axis_index(name) for name in ("x", "y", "z", "c"))
    position = (z * NY + y) * NC + c
    x_scalar = x.astype(jnp.int32).reshape(1)
    past = history.reshape(4, BLKS, B, B)
    coupling = inter[:, 0]

    lists = jnp.broadcast_to(dest_blocks[:, 0][None], (NX, 4, 16))
    metas = exchange(lists, "x")

    older = shift(past[3], "x", 1)
    sources = src_lists.swapaxes(2, 3)
    (sent,) = parcels(x_scalar, sources, past, coupling, False)
    sent = after(sent, older, metas)
    crossed = exchange(sent, "x")
    older = jnp.where(x == 0, jnp.zeros_like(older), after(older, sent))
    later_past = jnp.concatenate([older[None], past[:3]], 0)
    later_sent = parcels(x_scalar, sources, later_past, coupling, True)

    metas = after(metas, sent).reshape(NX, 64)
    targets = jnp.stack([metas, shift(metas, "c", 1)])
    late_targets = jnp.stack(spread(targets[:, 0, :16], "y"), axis=1)

    def place_of(target):
        device = target // BLKS
        inner = device // NC // NY * BLKS + target % BLKS
        return device % NC == c, device // NC % NY, inner

    same, across, inner = place_of(targets)
    places = jnp.where(same, across * 64 + inner, 256).reshape(512)
    same, across, inner = place_of(late_targets)
    late_places = jnp.where(same & (across == y), inner, 64).reshape(128)

    by_distance = places.reshape(2, NX, 64)[:, (x - jnp.arange(NX)) % NX].reshape(512)
    newest = after(coupling, sent)[0].swapaxes(2, 3).reshape(16, 4 * B, B)
    crossed = after(crossed, later_sent, places, by_distance, late_places, newest)
    crossed = crossed.reshape(256, RW, B)
    dense = place(places, [crossed, shift(crossed, "c", 1)])
    halves = exchange(dense, "y")
    later_sent = after(later_sent, crossed)
    steps = (0, 1, 2, -1)
    later_crossed = [later_sent[0]] + [
        shift(later_sent[n], "x", steps[n]) for n in range(1, NX)
    ]

    near, diag_inverse, excitation = after((near, diag_inverse, excitation), dense)
    near_t = near.swapaxes(2, 3).reshape(BLKS, 8 * B, B)
    inverse_t = diag_inverse.swapaxes(1, 2)
    incident = excitation.reshape(2, BLKS, B, B).swapaxes(2, 3)
    incident = lax.dynamic_slice_in_dim(incident, x * RW, RW, axis=2)
    ids = (nbr_ids - (position - 1) * BLKS).reshape(64)

    def one_sweep(current, drive):
        right = shift(current, BLK, -1)
        left = shift(current, BLK, 1)
        return sweep(ids, right, current, left, drive, near_t, inverse_t)

    later_own = shift(later_crossed[0], "c", 1)
    later_crossed = after(later_crossed, near_t, inverse_t, incident, ids, later_own)

    halves = after(halves, near_t, inverse_t, incident, ids)
    summed = add(halves)
    pieces = exchange(summed, "z")

    later_other = [later_own] + [shift(value, "c", 1) for value in later_crossed[1:]]
    later_dense = place(by_distance, later_crossed + later_other)

    pieces = after(pieces, later_dense)
    drive, current = first_solve(pieces, incident[0], inverse_t)
    for _ in range(SWEEPS):
        current = one_sweep(current, drive)
    later_halves = exchange(after(later_dense, current), "y")
    outputs = spread(current, "x")

    late = late_parcels(x_scalar, sources, outputs, newest)
    late = [late[0], shift(late[1], "x", 1), shift(late[2], "x", 2), shift(late[3], "x", -1)]
    mine = late[3]
    for n in range(NX - 2, -1, -1):
        mine = jnp.where(x == n, late[n], mine)
    mine = spread(after(mine, later_halves), "y")
    mine = mine + [shift(value, "c", 1) for value in mine]
    pieces = exchange(add_late(late_places, later_halves, mine), "z")
    drive, current = first_solve(pieces, incident[1], inverse_t)
    for _ in range(SWEEPS):
        current = one_sweep(current, drive)
    outputs = outputs + spread(current, "x")
    return finish(x_scalar, outputs).reshape(2, BLKS * B, B)


def solution(mesh):
    grid = Mesh(mesh.devices.reshape(NZ, NY, NC, NX), ("z", "y", "c", "x"))
    placed = (
        P(None, BLK, None),
        P("x", BLK, None),
        P("x", BLK, None, None, None, None),
        P("x", BLK, None, None),
        P("x", BLK, None),
        P(BLK, None, None, None),
        P(BLK, None, None),
        P(BLK, None),
    )
    return jax.shard_map(
        per_device, mesh=grid, in_specs=placed, out_specs=P(None, BLK, None), check_vma=False
    )
```
